32 devices in a mesh: seq: 16 (over z, y, x), head: 2 (over core).
Axes of the slice: x: 2, y: 2, z: 4, core: 2. Of those that a mesh axis runs over, the one named last changes fastest.
Arguments:
- events: bfloat16 [4096, 1024], P('seq'), may hold values from -6 to 6
- w_uvqk: bfloat16 [1024, 4, 1024], P('seq', None, 'head'), may hold values from -0.1875 to 0.1875
- w_out: bfloat16 [1024, 1024], P('head', 'seq'), may hold values from -0.1875 to 0.1875
- time_bias: bfloat16 [8, 128], P('head'), may hold values from -4 to 4
- stamps: int32 [4096], P('seq'), may hold values from 0 to 127, as said below
Outputs:
- mixed: bfloat16 [4096, 1024], P('seq', 'head')
The draws below stay inside these ranges and needn't reach their ends.
Inputs may be any that keep to these rules, and one draw needn't show every extreme that they name: stamps never fall along the events; the first is 0 and the last is 127.
All inputs are finite; a program needn't handle non-finite values.
Results may differ from the reference program's by a relative error of at most 0.0075.
Values may be sent and summed in bfloat16 or wider, within the bound.
No kernel may reach another device: no remote copies, remote signals or barrier semaphores. Data moves between devices by JAX's collectives and lax.ppermute only.
A program may use at most 128 MiB of HBM per device.

```python
import math
import jax
import jax.numpy as jnp
from jax import lax

D = 1024
H = 8
DH = 128
NB = 128
TOKENS = 4096


def draw_stamps(key, part):
    key = jax.random.fold_in(key, 1)
    order = jax.random.permutation(key, TOKENS - 1)
    marks = jnp.zeros((TOKENS,), jnp.int32).at[order[:NB - 1] + 1].set(1)
    return jnp.cumsum(marks).astype(jnp.int32)


def block_scale(stream_key, extent, shards, low, high):
    loudness, own = 1.0, jax.random.fold_in(stream_key, 6)
    for dim, parts in shards:
        steps = jnp.exp(jax.random.uniform(jax.random.fold_in(own, dim), (parts,), jnp.float32, low / len(shards), high / len(shards)))
        loudness = loudness * jnp.repeat(steps, extent[dim] // parts).reshape([-1 if axis == dim else 1 for axis in range(len(extent))])
    return loudness


def bell_draw(own_key, shape, deviation, reach, shards=(), kind=jnp.bfloat16):
    drawn = deviation * jax.random.normal(own_key, shape, jnp.float32)
    if shards:
        drawn = drawn * block_scale(own_key, shape, shards, -0.22, 0.18)
    return jnp.clip(drawn, -reach, reach).astype(kind)


def setup_inputs(seed: int = 0) -> dict:
    arg_keys = jax.random.split(jax.random.key(seed), 6)
    return {
        "events": bell_draw(arg_keys[0], (TOKENS, D), 1.0, 6.0, ((0, 16),)),
        "w_uvqk": bell_draw(arg_keys[1], (D, 4, H * DH), D ** -0.5, 0.1875, ((0, 16), (2, 2))),
        "w_out": bell_draw(arg_keys[2], (H * DH, D), (H * DH) ** -0.5, 0.1875, ((0, 2), (1, 16))),
        "time_bias": bell_draw(arg_keys[3], (H, NB), 1.0, 4.0, ((0, 2),)),
        "stamps": draw_stamps(jax.random.fold_in(arg_keys[5], 71), 0),
    }


EPSILON = 1e-05

def layer_norm(inputs):
    centre = inputs - lax.optimization_barrier(jnp.mean(inputs, axis=-1, keepdims=True))
    spread = lax.optimization_barrier(jnp.mean(centre * centre, axis=-1, keepdims=True))
    return centre * lax.rsqrt(spread + EPSILON)

def reference(events, w_uvqk, w_out, time_bias, stamps):
    inputs = events.astype(jnp.float32)
    normed = layer_norm(inputs).astype(jnp.bfloat16)
    width = H * DH
    projected = jnp.dot(normed, w_uvqk.reshape(D, 4 * width), preferred_element_type=jnp.float32)
    activated = jax.nn.silu(projected).astype(jnp.bfloat16).reshape(TOKENS, 4, width)
    gate_u = activated[:, 0]
    block = math.gcd(TOKENS, 1024)
    blocks = TOKENS // block
    value_heads = activated[:, 1].astype(jnp.float32).reshape(blocks, block, H, DH)
    query_heads = activated[:, 2].astype(jnp.float32).reshape(blocks, block, H, DH)
    key_heads = activated[:, 3].astype(jnp.float32).reshape(blocks, block, H, DH)
    stamp_blocks = stamps.reshape(blocks, block)
    table = time_bias.astype(jnp.float32)
    scale = 1.0 / math.sqrt(DH)
    positions = jnp.arange(block, dtype=jnp.int32)

    def one_block(query_index):
        query_block = query_heads[query_index]
        query_stamp = stamp_blocks[query_index]

        def add_keys(key_index, total):
            key_block = key_heads[key_index]
            value_block = value_heads[key_index]
            key_stamp = stamp_blocks[key_index]
            scores = jnp.einsum('qhd,khd->hqk', query_block, key_block, precision=lax.Precision.HIGHEST)
            gap = jnp.clip(query_stamp[:, None] - key_stamp[None, :], 0, NB - 1)
            scores = scores * scale + table[:, gap]
            allowed = (key_index * block + positions)[None, :] <= (query_index * block + positions)[:, None]
            weights = jnp.where(allowed[None], jax.nn.silu(scores), 0.0).astype(jnp.bfloat16).astype(jnp.float32)
            return total + jnp.einsum('hqk,khd->qhd', weights, value_block, precision=lax.Precision.HIGHEST)
        return lax.fori_loop(0, query_index + 1, add_keys, jnp.zeros((block, H, DH), jnp.float32))
    attended = lax.map(one_block, jnp.arange(blocks, dtype=jnp.int32))
    attended = attended.reshape(TOKENS, width).astype(jnp.bfloat16)
    normed_out = layer_norm(attended.astype(jnp.float32))
    gated = (normed_out * gate_u.astype(jnp.float32)).astype(jnp.bfloat16)
    return (inputs + jnp.dot(gated, w_out, preferred_element_type=jnp.float32)).astype(jnp.bfloat16)
```

```python
import functools
import math

import jax
import jax.numpy as jnp
from jax import lax
from jax.experimental import pallas as pl
from jax.experimental.pallas import tpu as pltpu
from jax.sharding import PartitionSpec as P

EPSILON = 1e-05
PAD = 16
VMEM_LIMIT = 50 * 1024 * 1024
NT = (((1,), (1,)), ((), ()))


def half_silu(t):
    return t * (1.0 + jnp.tanh(t))


def normalise(x):
    centre = x - jnp.mean(x, axis=-1, keepdims=True)
    spread = jnp.mean(centre * centre, axis=-1, keepdims=True)
    return centre * lax.rsqrt(spread + EPSILON)


def onehot_rows(stamp_row, buckets):
    count = stamp_row.shape[1]
    level = lax.broadcasted_iota(jnp.int32, (buckets, count), 0).astype(jnp.float32)
    return jnp.where(level == stamp_row, 1.0, 0.0).T


def vmem(count):
    return [pl.BlockSpec(memory_space=pltpu.VMEM)] * count


def projection_kernel(lead, lines, ids, events, *refs):
    arrived = refs[: lead - 1]
    other, bias_row, own_msg = refs[lead - 1 : lead + 2]
    marks = refs[lead + 2 : 2 * lead + 1]
    weights = refs[2 * lead + 1 : 2 * lead + 1 + lines]
    kv_ref, q_ref, u_ref, wbuf, xbuf = refs[2 * lead + 1 + lines :]
    a, i, c = ids[0], ids[1], ids[2]
    rows, _ = events.shape
    half = rows // 2
    size = u_ref.shape[1]
    buckets = bias_row.shape[1]
    chunk = wbuf.shape[0] // (lead * lines)
    for j in range(lines):
        for k in range(lead):
            place = ((a ^ k) * lines + (i ^ j)) * chunk
            wbuf[pl.ds(pl.multiple_of(place, chunk), chunk), :] = weights[j][
                k * chunk : (k + 1) * chunk, :
            ]
    table = jnp.broadcast_to(bias_row[...], (buckets, buckets))
    table = pltpu.roll(table, 0, 1, stride=1, stride_axis=0).astype(jnp.bfloat16)
    scale = 0.5 / math.sqrt(size)
    stamp_rows = lax.broadcasted_iota(jnp.int32, (PAD, rows), 0)
    stamp_tile = jnp.zeros((PAD, rows), jnp.float32)
    for k in range(lead):
        if k == 0:
            x = events[...].astype(jnp.float32)
            mark = own_msg[chunk : chunk + PAD, :rows]
        else:
            xbuf[pl.ds(pl.multiple_of(c * half, half), half), :] = arrived[k - 1][...]
            xbuf[pl.ds(pl.multiple_of((1 - c) * half, half), half), :] = other[
                (k - 1) * half : k * half, :
            ]
            x = xbuf[...].astype(jnp.float32)
            mark = marks[k - 1][chunk : chunk + PAD, :rows]
        mark = mark.astype(jnp.float32)[0:1, :]
        normed = normalise(x).astype(jnp.bfloat16)
        product = jnp.dot(normed, wbuf[...], preferred_element_type=jnp.float32)
        active = half_silu(0.5 * product)
        base = pl.ds(pl.multiple_of((a ^ k) * rows, rows), rows)
        u_ref[base, :] = active[:, :size].astype(jnp.bfloat16)
        kv_ref[base, size : 2 * size] = active[:, size : 2 * size].astype(jnp.bfloat16)
        q_ref[base, :size] = (active[:, 2 * size : 3 * size] * scale).astype(jnp.bfloat16)
        kv_ref[base, :size] = active[:, 3 * size :].astype(jnp.bfloat16)
        chosen = onehot_rows(mark, buckets).astype(jnp.bfloat16)
        q_ref[base, size:] = jnp.dot(
            chosen, table, preferred_element_type=jnp.float32
        ).astype(jnp.bfloat16)
        stamp_tile = jnp.where(stamp_rows == (a ^ k), mark, stamp_tile)
    kv_ref[lead * rows :, :] = stamp_tile.astype(jnp.bfloat16)


def attention_kernel(lead, j, last, ids, q_ref, kv_ref, *refs):
    refs = list(refs)
    before = refs.pop(0) if j > 0 else None
    u_ref = refs.pop(0) if last else None
    outs, (kaug, total) = refs[:-2], refs[-2:]
    a, i = ids[0], ids[1]
    size = q_ref.shape[1] // 2
    rows = q_ref.shape[0] // lead
    buckets = q_ref.shape[1] - size
    kaug[:, :size] = kv_ref[: lead * rows, :size]
    marks = kv_ref[lead * rows :, :].astype(jnp.float32)
    for p in range(lead):
        kaug[p * rows : (p + 1) * rows, size:] = onehot_rows(marks[p : p + 1, :], buckets).astype(
            jnp.bfloat16
        )

    def visit(extra):
        for p in range(lead):
            block = slice(p * rows, (p + 1) * rows)
            count = (p + extra) * rows
            old = before[block, :] if before is not None else None
            if count == 0:
                total[block, :] = old if old is not None else jnp.zeros((rows, size), jnp.float32)
                continue
            t = lax.dot_general(
                q_ref[block, :], kaug[:count, :], NT, preferred_element_type=jnp.float32
            )
            weight = half_silu(t)
            if j == 0:
                row = lax.broadcasted_iota(jnp.int32, (rows, count), 0) + p * rows
                column = lax.broadcasted_iota(jnp.int32, (rows, count), 1)
                weight = jnp.where(column <= row, weight, 0.0)
            update = jnp.dot(
                weight.astype(jnp.bfloat16),
                kv_ref[:count, size:],
                preferred_element_type=jnp.float32,
            )
            total[block, :] = update if old is None else old + update

    if j == 0:
        visit(1)
    else:
        pl.when((i ^ j) < i)(lambda: visit(1))
        pl.when((i ^ j) > i)(lambda: visit(0))
    if last:
        for k in range(lead):
            base = pl.ds(pl.multiple_of((a ^ k) * rows, rows), rows)
            outs[k][:, :size] = total[base, :].astype(jnp.bfloat16)
            outs[k][:, size:] = u_ref[base, :]
    else:
        outs[0][...] = total[...]


def output_kernel(lead, lines, ids, events, kept, given, *refs):
    own = refs[:lead]
    other = refs[lead : 2 * lead]
    out_ref, gated, wbuf = refs[2 * lead :]
    a, i, c = ids[0], ids[1], ids[2]
    rows, share = out_ref.shape
    size = own[0].shape[1] // 2
    full = 2 * lead * size
    chunk = kept.shape[0] // (2 * lines)
    for k in range(2):
        for j in range(lines):
            place = (((a ^ k) & 1) * lines + (i ^ j)) * chunk
            source = slice((k * lines + j) * chunk, (k * lines + j + 1) * chunk)
            to = pl.ds(pl.multiple_of(place, chunk), chunk)
            wbuf[0, to, :] = kept[source, :]
            wbuf[1, to, :] = given[source, :]
    parts = [ref[:, :size].astype(jnp.float32) for ref in (*own, *other)]
    middle = functools.reduce(jnp.add, [jnp.sum(x, -1, keepdims=True) for x in parts]) / full
    parts = [x - middle for x in parts]
    spread = functools.reduce(jnp.add, [jnp.sum(x * x, -1, keepdims=True) for x in parts]) / full
    inverse = lax.rsqrt(spread + EPSILON)
    for side, group in enumerate((own, other)):
        for k in range(lead):
            value = parts[side * lead + k] * inverse * group[k][:, size:].astype(jnp.float32)
            place = pl.ds(pl.multiple_of((a ^ k) * size, size), size)
            gated[side, :, place] = value.astype(jnp.bfloat16)
    total = lax.dot_general(gated[0], wbuf[0], NT, preferred_element_type=jnp.float32)
    total += lax.dot_general(gated[1], wbuf[1], NT, preferred_element_type=jnp.float32)
    residual = events[:, pl.ds(pl.multiple_of(c * share, share), share)].astype(jnp.float32)
    out_ref[...] = (residual + total).astype(jnp.bfloat16)


def call(kernel, ins, outs, scratch, flops, transcendentals=0):
    size = sum(math.prod(x.shape) * x.dtype.itemsize for x in [*ins, *outs])
    return pl.pallas_call(
        kernel,
        out_shape=outs,
        in_specs=[pl.BlockSpec(memory_space=pltpu.SMEM)] + vmem(len(ins) - 1),
        out_specs=vmem(len(outs)),
        scratch_shapes=scratch,
        compiler_params=pltpu.CompilerParams(vmem_limit_bytes=VMEM_LIMIT),
        cost_estimate=pl.CostEstimate(
            flops=flops, bytes_accessed=size, transcendentals=transcendentals
        ),
    )(*ins)


def per_device(events, w_uvqk, w_out, time_bias, stamps):
    bf16, f32 = jnp.bfloat16, jnp.float32
    devices = lax.axis_size("seq")
    rows, width = events.shape
    lead = time_bias.shape[0]
    lines = devices // lead
    chunk = w_uvqk.shape[0]
    size = w_uvqk.shape[2] // lead
    share = width // lax.axis_size("head")
    half = rows // 2
    place, c = lax.axis_index("seq"), lax.axis_index("head")
    a, i = place // lines, place % lines
    ids = jnp.stack([a, i, c]).astype(jnp.int32)

    def exchange(x, flip):
        return lax.ppermute(x, "seq", [(t, t ^ flip) for t in range(devices)])

    def swap(x):
        return lax.ppermute(x, "head", [(0, 1), (1, 0)])

    def shape(*dims, dtype=bf16):
        return jax.ShapeDtypeStruct(dims, dtype)

    by_head = w_uvqk.reshape(chunk, 4, lead, size).transpose(2, 0, 1, 3).reshape(lead, chunk, -1)
    stamp_rows = jnp.pad(stamps.astype(bf16)[None, :], ((0, PAD - 1), (0, 4 * size - rows)))
    sent = [
        jnp.concatenate([lax.dynamic_index_in_dim(by_head, a ^ k, 0, False), stamp_rows])
        for k in range(lead)
    ]
    got = [exchange(sent[k], k * lines) for k in range(1, lead)]
    own_half = lax.dynamic_slice_in_dim(events, c * half, half, 0)
    arrived = [exchange(own_half, k * lines) for k in range(1, lead)]
    w_out_t = w_out.T
    stack = jnp.concatenate([x[:chunk] for x in [sent[0], *got]] + [w_out_t])
    stacks = [stack] + [exchange(stack, j) for j in range(1, lines)]
    other = swap(jnp.concatenate(arrived))
    bias_row = lax.dynamic_index_in_dim(time_bias, a, 0, True).astype(f32) * 0.5
    bias_row = jnp.roll(bias_row[:, ::-1], 1, axis=1)

    span = lead * rows
    kv, queries, gate = call(
        functools.partial(projection_kernel, lead, lines),
        [ids, events, *arrived, other, bias_row, sent[0], *got, *stacks],
        [shape(span + PAD, 2 * size), shape(span, size + bias_row.shape[1]), shape(span, size)],
        [pltpu.VMEM((width, 4 * size), bf16), pltpu.VMEM((rows, width), bf16)],
        2 * span * width * 4 * size,
        span * 4 * size,
    )
    kvs = [kv] + [exchange(kv, j) for j in range(1, lines)]

    columns = jnp.concatenate([x[lead * chunk :] for x in stacks])
    shares = [columns] + [exchange(columns, k * lines) for k in range(1, lead)]
    low, high = jnp.concatenate(shares[: lead // 2]), jnp.concatenate(shares[lead // 2 :])
    mine = (a // (lead // 2)) == c
    kept = jnp.where(mine, low, high)
    given = swap(jnp.where(mine, high, low))

    total = None
    for j in range(lines):
        last = j == lines - 1
        ins = [ids, queries, kvs[j]] + ([total] if j else []) + ([gate] if last else [])
        outs = [shape(rows, 2 * size)] * lead if last else [shape(span, size, dtype=f32)]
        result = call(
            functools.partial(attention_kernel, lead, j, last),
            ins,
            outs,
            [pltpu.VMEM((span, queries.shape[1]), bf16), pltpu.VMEM((span, size), f32)],
            span * span * 3 * size,
            span * span // 2,
        )
        total = result[0]
    own = [result[0]] + [exchange(result[k], k * lines) for k in range(1, lead)]
    across = [swap(x) for x in own]
    return call(
        functools.partial(output_kernel, lead, lines),
        [ids, events, kept, given, *own, *across],
        [shape(rows, share)],
        [
            pltpu.VMEM((2, rows, lead * size), bf16),
            pltpu.VMEM((2, share, lead * size), bf16),
        ],
        2 * rows * width * share,
    )[0]


def solution(mesh):
    placed = (P("seq", None), P("seq", None, "head"), P("head", "seq"), P("head", None), P("seq"))
    return jax.shard_map(
        per_device, mesh=mesh, in_specs=placed, out_specs=P("seq", "head"), check_vma=False
    )
```

```python
import functools
import math

import jax
import jax.numpy as jnp
from jax import lax
from jax.experimental import pallas as pl
from jax.experimental.pallas import tpu as pltpu
from jax.sharding import PartitionSpec as P

EPSILON = 1e-05
PAD = 16
VMEM_LIMIT = 50 * 1024 * 1024
NT = (((1,), (1,)), ((), ()))


def half_silu(t):
    return t * (1.0 + jnp.tanh(t))


def normalise(x):
    centre = x - jnp.mean(x, axis=-1, keepdims=True)
    spread = jnp.mean(centre * centre, axis=-1, keepdims=True)
    return centre * lax.rsqrt(spread + EPSILON)


def onehot_rows(stamp_row, buckets):
    count = stamp_row.shape[1]
    level = lax.broadcasted_iota(jnp.int32, (buckets, count), 0).astype(jnp.float32)
    return jnp.where(level == stamp_row, 1.0, 0.0).T


def vmem(count):
    return [pl.BlockSpec(memory_space=pltpu.VMEM)] * count


def projection_kernel(lead, lines, ids, events, *refs):
    arrived = refs[: lead - 1]
    other, bias_row, own_msg = refs[lead - 1 : lead + 2]
    marks = refs[lead + 2 : 2 * lead + 1]
    weights = refs[2 * lead + 1 : 2 * lead + 1 + lines]
    kv_ref, q_ref, *u_refs = refs[2 * lead + 1 + lines : -2]
    wbuf, xbuf = refs[-2:]
    a, i, c = ids[0], ids[1], ids[2]
    rows, _ = events.shape
    half = rows // 2
    size = u_refs[0].shape[1]
    buckets = bias_row.shape[1]
    chunk = wbuf.shape[0] // (lead * lines)
    for j in range(lines):
        for k in range(lead):
            place = ((a ^ k) * lines + (i ^ j)) * chunk
            wbuf[pl.ds(pl.multiple_of(place, chunk), chunk), :] = weights[j][
                k * chunk : (k + 1) * chunk, :
            ]
    table = jnp.broadcast_to(bias_row[...], (buckets, buckets))
    table = pltpu.roll(table, 0, 1, stride=1, stride_axis=0).astype(jnp.bfloat16)
    scale = 0.5 / math.sqrt(size)
    stamp_rows = lax.broadcasted_iota(jnp.int32, (PAD, rows), 0)
    stamp_tile = jnp.zeros((PAD, rows), jnp.float32)
    for k in range(lead):
        if k == 0:
            x = events[...].astype(jnp.float32)
            mark = own_msg[chunk : chunk + PAD, :rows]
        else:
            xbuf[pl.ds(pl.multiple_of(c * half, half), half), :] = arrived[k - 1][...]
            xbuf[pl.ds(pl.multiple_of((1 - c) * half, half), half), :] = other[
                (k - 1) * half : k * half, :
            ]
            x = xbuf[...].astype(jnp.float32)
            mark = marks[k - 1][chunk : chunk + PAD, :rows]
        mark = mark.astype(jnp.float32)[0:1, :]
        normed = normalise(x).astype(jnp.bfloat16)
        product = jnp.dot(normed, wbuf[...], preferred_element_type=jnp.float32)
        active = half_silu(0.5 * product)
        base = pl.ds(pl.multiple_of((a ^ k) * rows, rows), rows)
        u_refs[k][...] = active[:, :size].astype(jnp.bfloat16)
        kv_ref[base, size : 2 * size] = active[:, size : 2 * size].astype(jnp.bfloat16)
        q_ref[base, :size] = (active[:, 2 * size : 3 * size] * scale).astype(jnp.bfloat16)
        kv_ref[base, :size] = active[:, 3 * size :].astype(jnp.bfloat16)
        chosen = onehot_rows(mark, buckets).astype(jnp.bfloat16)
        q_ref[base, size:] = jnp.dot(
            chosen, table, preferred_element_type=jnp.float32
        ).astype(jnp.bfloat16)
        stamp_tile = jnp.where(stamp_rows == (a ^ k), mark, stamp_tile)
    kv_ref[lead * rows :, :] = stamp_tile.astype(jnp.bfloat16)


def attention_kernel(lead, j, last, ids, q_ref, kv_ref, *refs):
    refs = list(refs)
    before = refs.pop(0) if j > 0 else None
    gates, refs = (refs[:lead], refs[lead:]) if last else ([], refs)
    outs, (kaug, total) = refs[:-2], refs[-2:]
    a, i = ids[0], ids[1]
    size = q_ref.shape[1] // 2
    rows = q_ref.shape[0] // lead
    buckets = q_ref.shape[1] - size
    kaug[:, :size] = kv_ref[: lead * rows, :size]
    marks = kv_ref[lead * rows :, :].astype(jnp.float32)
    for p in range(lead):
        kaug[p * rows : (p + 1) * rows, size:] = onehot_rows(marks[p : p + 1, :], buckets).astype(
            jnp.bfloat16
        )

    def visit(extra):
        for p in range(lead):
            block = slice(p * rows, (p + 1) * rows)
            count = (p + extra) * rows
            old = before[block, :] if before is not None else None
            if count == 0:
                total[block, :] = old if old is not None else jnp.zeros((rows, size), jnp.float32)
                continue
            t = lax.dot_general(
                q_ref[block, :], kaug[:count, :], NT, preferred_element_type=jnp.float32
            )
            weight = half_silu(t)
            if j == 0:
                row = lax.broadcasted_iota(jnp.int32, (rows, count), 0) + p * rows
                column = lax.broadcasted_iota(jnp.int32, (rows, count), 1)
                weight = jnp.where(column <= row, weight, 0.0)
            update = jnp.dot(
                weight.astype(jnp.bfloat16),
                kv_ref[:count, size:],
                preferred_element_type=jnp.float32,
            )
            total[block, :] = update if old is None else old + update

    if j == 0:
        visit(1)
    else:
        pl.when((i ^ j) < i)(lambda: visit(1))
        pl.when((i ^ j) > i)(lambda: visit(0))
    if last:
        for k in range(lead):
            base = pl.ds(pl.multiple_of((a ^ k) * rows, rows), rows)
            outs[k][:, :size] = total[base, :].astype(jnp.bfloat16)
            outs[k][:, size:] = gates[k][...]
    else:
        outs[0][...] = total[...]


def output_kernel(lead, lines, ids, events, kept, given, *refs):
    own = refs[:lead]
    other = refs[lead : 2 * lead]
    out_ref, gated, wbuf = refs[2 * lead :]
    a, i, c = ids[0], ids[1], ids[2]
    rows, share = out_ref.shape
    size = own[0].shape[1] // 2
    full = 2 * lead * size
    chunk = kept.shape[0] // (2 * lines)
    for k in range(2):
        for j in range(lines):
            place = (((a ^ k) & 1) * lines + (i ^ j)) * chunk
            source = slice((k * lines + j) * chunk, (k * lines + j + 1) * chunk)
            to = pl.ds(pl.multiple_of(place, chunk), chunk)
            wbuf[0, to, :] = kept[source, :]
            wbuf[1, to, :] = given[source, :]
    parts = [ref[:, :size].astype(jnp.float32) for ref in (*own, *other)]
    middle = functools.reduce(jnp.add, [jnp.sum(x, -1, keepdims=True) for x in parts]) / full
    parts = [x - middle for x in parts]
    spread = functools.reduce(jnp.add, [jnp.sum(x * x, -1, keepdims=True) for x in parts]) / full
    inverse = lax.rsqrt(spread + EPSILON)
    for side, group in enumerate((own, other)):
        for k in range(lead):
            value = parts[side * lead + k] * inverse * group[k][:, size:].astype(jnp.float32)
            place = pl.ds(pl.multiple_of((a ^ k) * size, size), size)
            gated[side, :, place] = value.astype(jnp.bfloat16)
    total = lax.dot_general(gated[0], wbuf[0], NT, preferred_element_type=jnp.float32)
    total += lax.dot_general(gated[1], wbuf[1], NT, preferred_element_type=jnp.float32)
    residual = events[:, pl.ds(pl.multiple_of(c * share, share), share)].astype(jnp.float32)
    out_ref[...] = (residual + total).astype(jnp.bfloat16)


def call(kernel, ins, outs, scratch, flops, transcendentals=0):
    size = sum(math.prod(x.shape) * x.dtype.itemsize for x in [*ins, *outs])
    return list(pl.pallas_call(
        kernel,
        out_shape=outs,
        in_specs=[pl.BlockSpec(memory_space=pltpu.SMEM)] + vmem(len(ins) - 1),
        out_specs=vmem(len(outs)),
        scratch_shapes=scratch,
        compiler_params=pltpu.CompilerParams(vmem_limit_bytes=VMEM_LIMIT),
        cost_estimate=pl.CostEstimate(
            flops=flops, bytes_accessed=size, transcendentals=transcendentals
        ),
    )(*ins))


def per_device(events, w_uvqk, w_out, time_bias, stamps):
    bf16, f32 = jnp.bfloat16, jnp.float32
    devices = lax.axis_size("seq")
    rows, width = events.shape
    lead = time_bias.shape[0]
    lines = devices // lead
    chunk = w_uvqk.shape[0]
    size = w_uvqk.shape[2] // lead
    share = width // lax.axis_size("head")
    half = rows // 2
    place, c = lax.axis_index("seq"), lax.axis_index("head")
    a, i = place // lines, place % lines
    ids = jnp.stack([a, i, c]).astype(jnp.int32)

    def exchange(x, flip):
        return lax.ppermute(x, "seq", [(t, t ^ flip) for t in range(devices)])

    def spread(x):
        held = [x]
        for k in range(1, lead):
            low = k & -k
            held.append(exchange(held[k ^ low], low * lines))
        return held

    def swap(x):
        return lax.ppermute(x, "head", [(0, 1), (1, 0)])

    def shape(*dims, dtype=bf16):
        return jax.ShapeDtypeStruct(dims, dtype)

    by_head = w_uvqk.reshape(chunk, 4, lead, size).transpose(2, 0, 1, 3).reshape(lead, chunk, -1)
    stamp_rows = jnp.pad(stamps.astype(bf16)[None, :], ((0, PAD - 1), (0, 4 * size - rows)))
    sent = [
        jnp.concatenate([lax.dynamic_index_in_dim(by_head, a ^ k, 0, False), stamp_rows])
        for k in range(lead)
    ]
    got = [exchange(sent[k], k * lines) for k in range(1, lead)]
    own_half = lax.dynamic_slice_in_dim(events, c * half, half, 0)
    own_half, got[0] = lax.optimization_barrier((own_half, got[0]))
    arrived = spread(own_half)[1:]
    w_out_t = w_out.T
    stack = jnp.concatenate([x[:chunk] for x in [sent[0], *got]] + [w_out_t])
    stacks = [stack] + [exchange(stack, j) for j in range(1, lines)]
    held = lax.optimization_barrier((*arrived, *stacks[1:]))
    arrived, stacks[1:] = list(held[: lead - 1]), held[lead - 1 :]
    other = swap(jnp.concatenate(arrived))
    bias_row = lax.dynamic_index_in_dim(time_bias, a, 0, True).astype(f32) * 0.5
    bias_row = jnp.roll(bias_row[:, ::-1], 1, axis=1)

    span = lead * rows
    kv, queries, *gates = call(
        functools.partial(projection_kernel, lead, lines),
        [ids, events, *arrived, other, bias_row, sent[0], *got, *stacks],
        [shape(span + PAD, 2 * size), shape(span, size + bias_row.shape[1])]
        + [shape(rows, size)] * lead,
        [pltpu.VMEM((width, 4 * size), bf16), pltpu.VMEM((rows, width), bf16)],
        2 * span * width * 4 * size,
        span * 4 * size,
    )

    def attend(j, total):
        last = j == lines - 1
        outs = [shape(rows, 2 * size)] * lead if last else [shape(span, size, dtype=f32)]
        return call(
            functools.partial(attention_kernel, lead, j, last),
            [ids, queries, kvs[j]] + ([total] if j else []) + (gates if last else []),
            outs,
            [pltpu.VMEM((span, queries.shape[1]), bf16), pltpu.VMEM((span, size), f32)],
            span * span * 3 * size,
            span * span // 2,
        )

    columns = jnp.concatenate([x[lead * chunk :] for x in stacks])
    columns, kv = lax.optimization_barrier((columns, kv))
    kvs = [kv] + [exchange(kv, j) for j in range(1, lines)]
    shares = spread(columns)
    low, high = jnp.concatenate(shares[: lead // 2]), jnp.concatenate(shares[lead // 2 :])
    mine = (a // (lead // 2)) == c
    kept = jnp.where(mine, low, high)
    given = swap(jnp.where(mine, high, low))

    result = [None]
    for j in range(lines):
        result = attend(j, result[0])
    own = [result[0]] + [exchange(result[k], k * lines) for k in range(1, lead)]
    across = [swap(x) for x in own]
    return call(
        functools.partial(output_kernel, lead, lines),
        [ids, events, kept, given, *own, *across],
        [shape(rows, share)],
        [
            pltpu.VMEM((2, rows, lead * size), bf16),
            pltpu.VMEM((2, share, lead * size), bf16),
        ],
        2 * rows * width * share,
    )[0]


def solution(mesh):
    placed = (P("seq", None), P("seq", None, "head"), P("head", "seq"), P("head", None), P("seq"))
    return jax.shard_map(
        per_device, mesh=mesh, in_specs=placed, out_specs=P("seq", "head"), check_vma=False
    )
```

```python
import functools
import math

import jax
import jax.numpy as jnp
from jax import lax
from jax.experimental import pallas as pl
from jax.experimental.pallas import tpu as pltpu
from jax.sharding import PartitionSpec as P

EPSILON = 1e-05
PAD = 16
VMEM_LIMIT = 50 * 1024 * 1024
NT = (((1,), (1,)), ((), ()))


def half_silu(t):
    return t * (1.0 + jnp.tanh(t))


def normalise(x):
    centre = x - jnp.mean(x, axis=-1, keepdims=True)
    spread = jnp.mean(centre * centre, axis=-1, keepdims=True)
    return centre * lax.rsqrt(spread + EPSILON)


def onehot_rows(stamp_row, buckets):
    count = stamp_row.shape[1]
    level = lax.broadcasted_iota(jnp.int32, (buckets, count), 0).astype(jnp.float32)
    return jnp.where(level == stamp_row, 1.0, 0.0).T


def vmem(count):
    return [pl.BlockSpec(memory_space=pltpu.VMEM)] * count


def norm_kernel(ids, events, normed_ref, half_ref):
    half = half_ref.shape[0]
    normed_ref[...] = normalise(events[...].astype(jnp.float32)).astype(jnp.bfloat16)
    half_ref[...] = normed_ref[pl.ds(pl.multiple_of(ids[2] * half, half), half), :]


def gather_weights(lead, lines, a, i, weights, wbuf, slices):
    size = wbuf.shape[1] // len(slices)
    chunk = wbuf.shape[0] // (lead * lines)
    for j in range(lines):
        for k in range(lead):
            place = ((a ^ k) * lines + (i ^ j)) * chunk
            to = pl.ds(pl.multiple_of(place, chunk), chunk)
            for n, part in enumerate(slices):
                wbuf[to, n * size : (n + 1) * size] = weights[j][
                    k * chunk : (k + 1) * chunk, part * size : (part + 1) * size
                ]


def keys_kernel(lead, lines, ids, normed, own_msg, *refs):
    arrived, refs = refs[: lead - 1], refs[lead - 1 :]
    others, refs = refs[: lead - 1], refs[lead - 1 :]
    marks, refs = refs[: lead - 1], refs[lead - 1 :]
    weights, (kv_ref, all_ref, columns_ref, wbuf) = refs[:lines], refs[lines:]
    a, i, c = ids[0], ids[1], ids[2]
    rows = normed.shape[0]
    half = rows // 2
    size = wbuf.shape[1] // 2
    chunk = wbuf.shape[0] // (lead * lines)
    gather_weights(lead, lines, a, i, weights, wbuf, (3, 1))
    for j in range(lines):
        columns_ref[j * chunk : (j + 1) * chunk, :] = weights[j][lead * chunk :, :]
    all_ref[pl.ds(pl.multiple_of(a * rows, rows), rows), :] = normed[...]
    for k in range(1, lead):
        for side, block in ((c, arrived[k - 1]), (1 - c, others[k - 1])):
            place = (a ^ k) * rows + side * half
            all_ref[pl.ds(pl.multiple_of(place, half), half), :] = block[...]
    for p in range(lead):
        block = slice(p * rows, (p + 1) * rows)
        product = jnp.dot(all_ref[block, :], wbuf[...], preferred_element_type=jnp.float32)
        kv_ref[block, :] = half_silu(0.5 * product).astype(jnp.bfloat16)
    stamp_rows = lax.broadcasted_iota(jnp.int32, (PAD, rows), 0)
    stamp_tile = jnp.zeros((PAD, rows), jnp.float32)
    for k, ref in enumerate((own_msg, *marks)):
        mark = ref[chunk : chunk + PAD, :rows].astype(jnp.float32)[0:1, :]
        stamp_tile = jnp.where(stamp_rows == (a ^ k), mark, stamp_tile)
    kv_ref[lead * rows :, :] = stamp_tile.astype(jnp.bfloat16)


def queries_kernel(lead, lines, ids, normed_all, time_bias, kv_ref, *refs):
    weights, (q_ref, *gate_refs, wbuf, ubuf) = refs[:lines], refs[lines:]
    a, i = ids[0], ids[1]
    size = wbuf.shape[1] // 2
    buckets = time_bias.shape[1]
    chunk = wbuf.shape[0] // (lead * lines)
    rows = normed_all.shape[0] // lead
    gather_weights(lead, lines, a, i, weights, wbuf, (2, 0))
    bias = time_bias[...].astype(jnp.float32) * 0.5
    picked = lax.broadcasted_iota(jnp.int32, bias.shape, 0) == a
    bias = jnp.sum(jnp.where(picked, bias, 0.0), axis=0, keepdims=True)
    table = jnp.broadcast_to(bias, (buckets, buckets))
    table = pltpu.roll(table, 0, 1, stride=1, stride_axis=0).astype(jnp.bfloat16)
    marks = kv_ref[lead * rows :, :].astype(jnp.float32)
    scale = 0.5 / math.sqrt(size)
    for p in range(lead):
        block = slice(p * rows, (p + 1) * rows)
        product = jnp.dot(normed_all[block, :], wbuf[...], preferred_element_type=jnp.float32)
        active = half_silu(0.5 * product)
        q_ref[block, :size] = (active[:, :size] * scale).astype(jnp.bfloat16)
        ubuf[block, :] = active[:, size:].astype(jnp.bfloat16)
        chosen = onehot_rows(marks[p : p + 1, :], buckets).astype(jnp.bfloat16)
        q_ref[block, size:] = lax.dot_general(
            chosen, table, NT, preferred_element_type=jnp.float32
        ).astype(jnp.bfloat16)
    for k in range(lead):
        gate_refs[k][...] = ubuf[pl.ds(pl.multiple_of((a ^ k) * rows, rows), rows), :]


def attention_kernel(lead, j, last, pieces, ids, q_ref, *refs):
    refs = list(refs)
    kv_refs, refs = refs[:pieces], refs[pieces:]
    before = refs.pop(0) if j > 0 else None
    gates, refs = (refs[:lead], refs[lead:]) if last else ([], refs)
    outs, (kaug, values, total) = refs[:-3], refs[-3:]
    a, i = ids[0], ids[1]
    size = q_ref.shape[1] // 2
    rows = q_ref.shape[0] // lead
    buckets = q_ref.shape[1] - size
    span = lead * rows // pieces
    for n, ref in enumerate(kv_refs):
        kaug[n * span : (n + 1) * span, :size] = ref[:span, :size]
        if pieces > 1:
            values[n * span : (n + 1) * span, :] = ref[:span, size:]
    marks = kv_refs[-1][span:, :].astype(jnp.float32)
    for p in range(lead):
        kaug[p * rows : (p + 1) * rows, size:] = onehot_rows(marks[p : p + 1, :], buckets).astype(
            jnp.bfloat16
        )

    def visit(extra):
        for p in range(lead):
            block = slice(p * rows, (p + 1) * rows)
            count = (p + extra) * rows
            old = before[block, :] if before is not None else None
            if count == 0:
                total[block, :] = old if old is not None else jnp.zeros((rows, size), jnp.float32)
                continue
            t = lax.dot_general(
                q_ref[block, :], kaug[:count, :], NT, preferred_element_type=jnp.float32
            )
            weight = half_silu(t)
            if j == 0:
                row = lax.broadcasted_iota(jnp.int32, (rows, count), 0) + p * rows
                column = lax.broadcasted_iota(jnp.int32, (rows, count), 1)
                weight = jnp.where(column <= row, weight, 0.0)
            update = jnp.dot(
                weight.astype(jnp.bfloat16),
                values[:count, :] if pieces > 1 else kv_refs[0][:count, size:],
                preferred_element_type=jnp.float32,
            )
            total[block, :] = update if old is None else old + update

    if j == 0:
        visit(1)
    else:
        pl.when((i ^ j) < i)(lambda: visit(1))
        pl.when((i ^ j) > i)(lambda: visit(0))
    if last:
        for k in range(lead):
            base = pl.ds(pl.multiple_of((a ^ k) * rows, rows), rows)
            outs[k][:, :size] = total[base, :].astype(jnp.bfloat16)
            outs[k][:, size:] = gates[k][...]
    else:
        outs[0][...] = total[...]


def parcel_kernel(lead, ids, *refs):
    columns, (kept_ref, give_ref) = refs[:lead], refs[lead:]
    height = columns[0].shape[0]

    def place(low_ref, high_ref):
        for n in range(lead // 2):
            low_ref[n * height : (n + 1) * height, :] = columns[n][...]
            high_ref[n * height : (n + 1) * height, :] = columns[lead // 2 + n][...]

    mine = ids[0] // (lead // 2) == ids[2]
    pl.when(mine)(lambda: place(kept_ref, give_ref))
    pl.when(jnp.logical_not(mine))(lambda: place(give_ref, kept_ref))


def output_kernel(lead, lines, ids, events, kept, given, *refs):
    own, refs = refs[:lead], refs[lead:]
    other, refs = refs[:lead], refs[lead:]
    out_ref, gated, wbuf = refs
    a, i, c = ids[0], ids[1], ids[2]
    rows, share = out_ref.shape
    size = own[0].shape[1] // 2
    full = 2 * lead * size
    chunk = kept.shape[0] // (2 * lines)
    for k in range(2):
        for j in range(lines):
            place = (((a ^ k) & 1) * lines + (i ^ j)) * chunk
            source = slice((k * lines + j) * chunk, (k * lines + j + 1) * chunk)
            to = pl.ds(pl.multiple_of(place, chunk), chunk)
            wbuf[0, to, :] = kept[source, :]
            wbuf[1, to, :] = given[source, :]
    parts = [ref[:, :size].astype(jnp.float32) for ref in (*own, *other)]
    middle = functools.reduce(jnp.add, [jnp.sum(x, -1, keepdims=True) for x in parts]) / full
    parts = [x - middle for x in parts]
    spread = functools.reduce(jnp.add, [jnp.sum(x * x, -1, keepdims=True) for x in parts]) / full
    inverse = lax.rsqrt(spread + EPSILON)
    for side, group in enumerate((own, other)):
        for k in range(lead):
            value = parts[side * lead + k] * inverse * group[k][:, size:].astype(jnp.float32)
            place = pl.ds(pl.multiple_of((a ^ k) * size, size), size)
            gated[side, :, place] = value.astype(jnp.bfloat16)
    total = lax.dot_general(gated[0], wbuf[0], NT, preferred_element_type=jnp.float32)
    total += lax.dot_general(gated[1], wbuf[1], NT, preferred_element_type=jnp.float32)
    residual = events[:, pl.ds(pl.multiple_of(c * share, share), share)].astype(jnp.float32)
    out_ref[...] = (residual + total).astype(jnp.bfloat16)


def call(kernel, ins, outs, scratch):
    return list(pl.pallas_call(
        kernel,
        out_shape=outs,
        in_specs=[pl.BlockSpec(memory_space=pltpu.SMEM)] + vmem(len(ins) - 1),
        out_specs=vmem(len(outs)),
        scratch_shapes=scratch,
        compiler_params=pltpu.CompilerParams(vmem_limit_bytes=VMEM_LIMIT),
        cost_estimate=pl.CostEstimate(flops=1, bytes_accessed=1, transcendentals=0),
    )(*ins))


def per_device(events, w_uvqk, w_out, time_bias, stamps):
    bf16, f32 = jnp.bfloat16, jnp.float32
    devices = lax.axis_size("seq")
    rows, width = events.shape
    lead = time_bias.shape[0]
    lines = devices // lead
    chunk = w_uvqk.shape[0]
    size = w_uvqk.shape[2] // lead
    share = width // lax.axis_size("head")
    half = rows // 2
    place, c = lax.axis_index("seq"), lax.axis_index("head")
    a, i = place // lines, place % lines
    ids = jnp.stack([a, i, c]).astype(jnp.int32)

    def exchange(x, flip):
        return lax.ppermute(x, "seq", [(t, t ^ flip) for t in range(devices)])

    def swap(x):
        return lax.ppermute(x, "head", [(0, 1), (1, 0)])

    def shape(*dims, dtype=bf16):
        return jax.ShapeDtypeStruct(dims, dtype)

    by_head = w_uvqk.reshape(chunk, 4, lead, size).transpose(2, 0, 1, 3).reshape(lead, chunk, -1)
    stamp_rows = jnp.pad(stamps.astype(bf16)[None, :], ((0, PAD - 1), (0, 4 * size - rows)))
    sent = [
        jnp.concatenate([lax.dynamic_index_in_dim(by_head, a ^ k, 0, False), stamp_rows])
        for k in range(lead)
    ]
    got = [exchange(sent[k], k * lines) for k in range(1, lead)]
    normed, own_half = call(
        norm_kernel,
        [ids, events],
        [shape(rows, width), shape(half, width)],
        [],
    )
    own_half, got[0] = lax.optimization_barrier((own_half, got[0]))
    near, far = exchange(own_half, lines), exchange(own_half, 2 * lines)
    near, relayed = lax.optimization_barrier((near, far))
    arrived = [near, far, exchange(relayed, lines)]
    stack = jnp.concatenate([x[:chunk] for x in [sent[0], *got]] + [w_out.T])
    stacks = [stack] + [exchange(stack, j) for j in range(1, lines)]
    others = [swap(x) for x in arrived[:-1]]
    *stacks[1:], last_half = lax.optimization_barrier((*stacks[1:], arrived[-1]))
    arrived[-1] = last_half
    others.append(swap(last_half))

    span = lead * rows
    kv, normed_all, columns = call(
        functools.partial(keys_kernel, lead, lines),
        [ids, normed, sent[0], *arrived, *others, *got, *stacks],
        [shape(span + PAD, 2 * size), shape(span, width), shape(lines * chunk, w_out.shape[0])],
        [pltpu.VMEM((width, 2 * size), bf16)],
    )
    direct = [exchange(kv, j) for j in ((1, 2) if lines == 4 else range(1, lines))]
    near, far = exchange(columns, lines), exchange(columns, 2 * lines)
    queries, *gates = call(
        functools.partial(queries_kernel, lead, lines),
        [ids, normed_all, time_bias, kv, *stacks],
        [shape(span, size + time_bias.shape[1])] + [shape(rows, size)] * lead,
        [pltpu.VMEM((width, 2 * size), bf16), pltpu.VMEM((span, size), bf16)],
    )

    def attend(j, total):
        last = j == lines - 1
        outs = [shape(rows, 2 * size)] * lead if last else [shape(span, size, dtype=f32)]
        return call(
            functools.partial(attention_kernel, lead, j, last, len(kvs[j])),
            [ids, queries, *kvs[j]] + ([total] if j else []) + (gates if last else []),
            outs,
            [
                pltpu.VMEM((span, queries.shape[1]), bf16),
                pltpu.VMEM((span, size), bf16),
                pltpu.VMEM((span, size), f32),
            ],
        )

    kvs = [[kv]] + [[x] for x in direct]
    result = attend(0, None)
    *direct, far, near, result[0] = lax.optimization_barrier((*direct, far, near, result[0]))
    kvs = [[kv]] + [[x] for x in direct]
    if lines == 4:
        part = span // 2
        kvs.append([exchange(direct[1][:part], 1), exchange(direct[0][part:], 2)])
    relayed = exchange(far, lines)
    for j in range(1, lines):
        result = attend(j, result[0])
    relayed, result[0] = lax.optimization_barrier((relayed, result[0]))
    own = [result[0]] + [exchange(result[k], k * lines) for k in range(1, lead)]
    across = [swap(x) for x in own]
    parcel = shape(2 * lines * chunk, w_out.shape[0])
    kept, given = call(
        functools.partial(parcel_kernel, lead),
        [ids, columns, near, far, relayed],
        [parcel, parcel],
        [],
    )
    given = swap(given)
    return call(
        functools.partial(output_kernel, lead, lines),
        [ids, events, kept, given, *own, *across],
        [shape(rows, share)],
        [
            pltpu.VMEM((2, rows, lead * size), bf16),
            pltpu.VMEM((2, share, lead * size), bf16),
        ],
    )[0]


def solution(mesh):
    placed = (P("seq", None), P("seq", None, "head"), P("head", "seq"), P("head", None), P("seq"))
    return jax.shard_map(
        per_device, mesh=mesh, in_specs=placed, out_specs=P("seq", "head"), check_vma=False
    )
```

```python
import functools
import math

import jax
import jax.numpy as jnp
from jax import lax
from jax.experimental import pallas as pl
from jax.experimental.pallas import tpu as pltpu
from jax.sharding import PartitionSpec as P

EPSILON = 1e-05
PAD = 16
VMEM_LIMIT = 50 * 1024 * 1024
NT = (((1,), (1,)), ((), ()))


def half_silu(t):
    return t * (1.0 + jnp.tanh(t))


def normalise(x):
    centre = x - jnp.mean(x, axis=-1, keepdims=True)
    spread = jnp.mean(centre * centre, axis=-1, keepdims=True)
    return centre * lax.rsqrt(spread + EPSILON)


def onehot_rows(stamp_row, buckets):
    count = stamp_row.shape[1]
    level = lax.broadcasted_iota(jnp.int32, (buckets, count), 0).astype(jnp.float32)
    return jnp.where(level == stamp_row, 1.0, 0.0).T


def vmem(count):
    return [pl.BlockSpec(memory_space=pltpu.VMEM)] * count


def norm_kernel(ids, events, normed_ref, half_ref):
    half = half_ref.shape[0]
    normed_ref[...] = normalise(events[...].astype(jnp.float32)).astype(jnp.bfloat16)
    half_ref[...] = normed_ref[pl.ds(pl.multiple_of(ids[2] * half, half), half), :]


def gather_weights(lead, lines, a, i, weights, wbuf, slices):
    size = wbuf.shape[1] // len(slices)
    chunk = wbuf.shape[0] // (lead * lines)
    for j in range(lines):
        for k in range(lead):
            place = ((a ^ k) * lines + (i ^ j)) * chunk
            to = pl.ds(pl.multiple_of(place, chunk), chunk)
            for n, part in enumerate(slices):
                wbuf[to, n * size : (n + 1) * size] = weights[j][
                    k * chunk : (k + 1) * chunk, part * size : (part + 1) * size
                ]


def keys_kernel(lead, lines, ids, normed, own_msg, *refs):
    arrived, refs = refs[: lead - 1], refs[lead - 1 :]
    others, refs = refs[: lead - 1], refs[lead - 1 :]
    marks, refs = refs[: lead - 1], refs[lead - 1 :]
    weights, (kv_ref, all_ref, columns_ref, wbuf) = refs[:lines], refs[lines:]
    a, i, c = ids[0], ids[1], ids[2]
    rows = normed.shape[0]
    half = rows // 2
    size = wbuf.shape[1] // 2
    chunk = wbuf.shape[0] // (lead * lines)
    gather_weights(lead, lines, a, i, weights, wbuf, (3, 1))
    for j in range(lines):
        columns_ref[j * chunk : (j + 1) * chunk, :] = weights[j][lead * chunk :, :]
    all_ref[pl.ds(pl.multiple_of(a * rows, rows), rows), :] = normed[...]
    for k in range(1, lead):
        for side, block in ((c, arrived[k - 1]), (1 - c, others[k - 1])):
            place = (a ^ k) * rows + side * half
            all_ref[pl.ds(pl.multiple_of(place, half), half), :] = block[...]
    for p in range(lead):
        block = slice(p * rows, (p + 1) * rows)
        product = jnp.dot(all_ref[block, :], wbuf[...], preferred_element_type=jnp.float32)
        kv_ref[block, :] = half_silu(0.5 * product).astype(jnp.bfloat16)
    stamp_rows = lax.broadcasted_iota(jnp.int32, (PAD, rows), 0)
    stamp_tile = jnp.zeros((PAD, rows), jnp.float32)
    for k, ref in enumerate((own_msg, *marks)):
        mark = ref[chunk : chunk + PAD, :rows].astype(jnp.float32)[0:1, :]
        stamp_tile = jnp.where(stamp_rows == (a ^ k), mark, stamp_tile)
    kv_ref[lead * rows :, :] = stamp_tile.astype(jnp.bfloat16)


def queries_kernel(lead, lines, ids, normed_all, time_bias, kv_ref, *refs):
    weights, (q_ref, *gate_refs, wbuf, ubuf) = refs[:lines], refs[lines:]
    a, i = ids[0], ids[1]
    size = wbuf.shape[1] // 2
    buckets = time_bias.shape[1]
    chunk = wbuf.shape[0] // (lead * lines)
    rows = normed_all.shape[0] // lead
    gather_weights(lead, lines, a, i, weights, wbuf, (2, 0))
    bias = time_bias[...].astype(jnp.float32) * 0.5
    picked = lax.broadcasted_iota(jnp.int32, bias.shape, 0) == a
    bias = jnp.sum(jnp.where(picked, bias, 0.0), axis=0, keepdims=True)
    table = jnp.broadcast_to(bias, (buckets, buckets))
    table = pltpu.roll(table, 0, 1, stride=1, stride_axis=0).astype(jnp.bfloat16)
    marks = kv_ref[lead * rows :, :].astype(jnp.float32)
    scale = 0.5 / math.sqrt(size)
    for p in range(lead):
        block = slice(p * rows, (p + 1) * rows)
        product = jnp.dot(normed_all[block, :], wbuf[...], preferred_element_type=jnp.float32)
        active = half_silu(0.5 * product)
        q_ref[block, :size] = (active[:, :size] * scale).astype(jnp.bfloat16)
        ubuf[block, :] = active[:, size:].astype(jnp.bfloat16)
        chosen = onehot_rows(marks[p : p + 1, :], buckets).astype(jnp.bfloat16)
        q_ref[block, size:] = lax.dot_general(
            chosen, table, NT, preferred_element_type=jnp.float32
        ).astype(jnp.bfloat16)
    for k in range(lead):
        gate_refs[k][...] = ubuf[pl.ds(pl.multiple_of((a ^ k) * rows, rows), rows), :]


def attention_kernel(lead, j, last, pieces, ids, q_ref, *refs):
    refs = list(refs)
    kv_refs, refs = refs[:pieces], refs[pieces:]
    before = refs.pop(0) if j > 0 else None
    gates, refs = (refs[:lead], refs[lead:]) if last else ([], refs)
    outs, (kaug, values, total) = refs[:-3], refs[-3:]
    a, i = ids[0], ids[1]
    size = q_ref.shape[1] // 2
    rows = q_ref.shape[0] // lead
    buckets = q_ref.shape[1] - size
    span = lead * rows // pieces
    for n, ref in enumerate(kv_refs):
        kaug[n * span : (n + 1) * span, :size] = ref[:span, :size]
        if pieces > 1:
            values[n * span : (n + 1) * span, :] = ref[:span, size:]
    marks = kv_refs[-1][span:, :].astype(jnp.float32)
    for p in range(lead):
        kaug[p * rows : (p + 1) * rows, size:] = onehot_rows(marks[p : p + 1, :], buckets).astype(
            jnp.bfloat16
        )

    def visit(extra):
        for p in range(lead):
            block = slice(p * rows, (p + 1) * rows)
            count = (p + extra) * rows
            old = before[block, :] if before is not None else None
            if count == 0:
                total[block, :] = old if old is not None else jnp.zeros((rows, size), jnp.float32)
                continue
            t = lax.dot_general(
                q_ref[block, :], kaug[:count, :], NT, preferred_element_type=jnp.float32
            )
            weight = half_silu(t)
            if j == 0:
                row = lax.broadcasted_iota(jnp.int32, (rows, count), 0) + p * rows
                column = lax.broadcasted_iota(jnp.int32, (rows, count), 1)
                weight = jnp.where(column <= row, weight, 0.0)
            update = jnp.dot(
                weight.astype(jnp.bfloat16),
                values[:count, :] if pieces > 1 else kv_refs[0][:count, size:],
                preferred_element_type=jnp.float32,
            )
            total[block, :] = update if old is None else old + update

    if j == 0:
        visit(1)
    else:
        pl.when((i ^ j) < i)(lambda: visit(1))
        pl.when((i ^ j) > i)(lambda: visit(0))
    if last:
        for k in range(lead):
            base = pl.ds(pl.multiple_of((a ^ k) * rows, rows), rows)
            outs[k][:, :size] = total[base, :].astype(jnp.bfloat16)
            outs[k][:, size:] = gates[k][...]
    else:
        outs[0][...] = total[...]


def parcel_kernel(lead, lines, ids, *refs):
    columns, (kept_ref, give_ref) = refs[:lead], refs[lead:]
    a, i, c = ids[0], ids[1], ids[2]
    chunk = columns[0].shape[0] // lines
    parts = lead // 2

    def place(low_ref, high_ref):
        for n, ref in enumerate(columns):
            target = low_ref if n < parts else high_ref
            for j in range(lines):
                to = (((a ^ n) % parts) * lines + (i ^ j)) * chunk
                target[pl.ds(pl.multiple_of(to, chunk), chunk), :] = ref[
                    j * chunk : (j + 1) * chunk, :
                ]

    mine = a // parts == c
    pl.when(mine)(lambda: place(kept_ref, give_ref))
    pl.when(jnp.logical_not(mine))(lambda: place(give_ref, kept_ref))


def output_kernel(lead, ids, events, kept, given, *refs):
    own, refs = refs[:lead], refs[lead:]
    other, refs = refs[:lead], refs[lead:]
    out_ref, gated = refs
    a, c = ids[0], ids[2]
    rows, share = out_ref.shape
    size = own[0].shape[1] // 2
    full = 2 * lead * size
    parts = [ref[:, :size].astype(jnp.float32) for ref in (*own, *other)]
    middle = functools.reduce(jnp.add, [jnp.sum(x, -1, keepdims=True) for x in parts]) / full
    parts = [x - middle for x in parts]
    spread = functools.reduce(jnp.add, [jnp.sum(x * x, -1, keepdims=True) for x in parts]) / full
    inverse = lax.rsqrt(spread + EPSILON)
    for side, group in enumerate((own, other)):
        for k in range(lead):
            value = parts[side * lead + k] * inverse * group[k][:, size:].astype(jnp.float32)
            place = pl.ds(pl.multiple_of((a ^ k) * size, size), size)
            gated[side, :, place] = value.astype(jnp.bfloat16)
    total = lax.dot_general(gated[0], kept[...], NT, preferred_element_type=jnp.float32)
    total += lax.dot_general(gated[1], given[...], NT, preferred_element_type=jnp.float32)
    residual = events[:, pl.ds(pl.multiple_of(c * share, share), share)].astype(jnp.float32)
    out_ref[...] = (residual + total).astype(jnp.bfloat16)


def call(kernel, ins, outs, scratch):
    return list(pl.pallas_call(
        kernel,
        out_shape=outs,
        in_specs=[pl.BlockSpec(memory_space=pltpu.SMEM)] + vmem(len(ins) - 1),
        out_specs=vmem(len(outs)),
        scratch_shapes=scratch,
        compiler_params=pltpu.CompilerParams(vmem_limit_bytes=VMEM_LIMIT),
        cost_estimate=pl.CostEstimate(flops=1, bytes_accessed=1, transcendentals=0),
    )(*ins))


def per_device(events, w_uvqk, w_out, time_bias, stamps):
    bf16, f32 = jnp.bfloat16, jnp.float32
    devices = lax.axis_size("seq")
    rows, width = events.shape
    lead = time_bias.shape[0]
    lines = devices // lead
    chunk = w_uvqk.shape[0]
    size = w_uvqk.shape[2] // lead
    share = width // lax.axis_size("head")
    half = rows // 2
    place, c = lax.axis_index("seq"), lax.axis_index("head")
    a, i = place // lines, place % lines
    ids = jnp.stack([a, i, c]).astype(jnp.int32)

    def exchange(x, flip):
        return lax.ppermute(x, "seq", [(t, t ^ flip) for t in range(devices)])

    def swap(x):
        return lax.ppermute(x, "head", [(0, 1), (1, 0)])

    def shape(*dims, dtype=bf16):
        return jax.ShapeDtypeStruct(dims, dtype)

    by_head = w_uvqk.reshape(chunk, 4, lead, size).transpose(2, 0, 1, 3).reshape(lead, chunk, -1)
    stamp_rows = jnp.pad(stamps.astype(bf16)[None, :], ((0, PAD - 1), (0, 4 * size - rows)))
    sent = [
        jnp.concatenate([lax.dynamic_index_in_dim(by_head, a ^ k, 0, False), stamp_rows])
        for k in range(lead)
    ]
    got = [exchange(sent[k], k * lines) for k in range(1, lead)]
    normed, own_half = call(
        norm_kernel,
        [ids, events],
        [shape(rows, width), shape(half, width)],
        [],
    )
    own_half, got[0] = lax.optimization_barrier((own_half, got[0]))
    near, far = exchange(own_half, lines), exchange(own_half, 2 * lines)
    near, relayed = lax.optimization_barrier((near, far))
    arrived = [near, far, exchange(relayed, lines)]
    stack = jnp.concatenate([x[:chunk] for x in [sent[0], *got]] + [w_out.T])
    stacks = [stack] + [exchange(stack, j) for j in range(1, lines)]
    others = [swap(x) for x in arrived[:-1]]
    *stacks[1:], last_half = lax.optimization_barrier((*stacks[1:], arrived[-1]))
    arrived[-1] = last_half
    others.append(swap(last_half))

    span = lead * rows
    kv, normed_all, columns = call(
        functools.partial(keys_kernel, lead, lines),
        [ids, normed, sent[0], *arrived, *others, *got, *stacks],
        [shape(span + PAD, 2 * size), shape(span, width), shape(lines * chunk, w_out.shape[0])],
        [pltpu.VMEM((width, 2 * size), bf16)],
    )
    direct = [exchange(kv, j) for j in ((1, 2) if lines == 4 else range(1, lines))]
    near, far = exchange(columns, lines), exchange(columns, 2 * lines)
    queries, *gates = call(
        functools.partial(queries_kernel, lead, lines),
        [ids, normed_all, time_bias, kv, *stacks],
        [shape(span, size + time_bias.shape[1])] + [shape(rows, size)] * lead,
        [pltpu.VMEM((width, 2 * size), bf16), pltpu.VMEM((span, size), bf16)],
    )

    def attend(j, total):
        last = j == lines - 1
        outs = [shape(rows, 2 * size)] * lead if last else [shape(span, size, dtype=f32)]
        return call(
            functools.partial(attention_kernel, lead, j, last, len(kvs[j])),
            [ids, queries, *kvs[j]] + ([total] if j else []) + (gates if last else []),
            outs,
            [
                pltpu.VMEM((span, queries.shape[1]), bf16),
                pltpu.VMEM((span, size), bf16),
                pltpu.VMEM((span, size), f32),
            ],
        )

    kvs = [[kv]] + [[x] for x in direct]
    result = attend(0, None)
    far, near, _ = lax.optimization_barrier((far, near, result[0]))
    *direct, result[0] = lax.optimization_barrier((*direct, result[0]))
    kvs = [[kv]] + [[x] for x in direct]
    if lines == 4:
        part = span // 2
        kvs.append([exchange(direct[1][:part], 1), exchange(direct[0][part:], 2)])
    relayed = exchange(far, lines)
    for j in range(1, lines):
        result = attend(j, result[0])
    relayed, result[0] = lax.optimization_barrier((relayed, result[0]))
    own = [result[0]] + [exchange(result[k], k * lines) for k in range(1, lead)]
    across = [swap(x) for x in own]
    parcel = shape(2 * lines * chunk, w_out.shape[0])
    kept, given = call(
        functools.partial(parcel_kernel, lead, lines),
        [ids, columns, near, far, relayed],
        [parcel, parcel],
        [],
    )
    given = swap(given)
    return call(
        functools.partial(output_kernel, lead),
        [ids, events, kept, given, *own, *across],
        [shape(rows, share)],
        [
            pltpu.VMEM((2, rows, lead * size), bf16),
        ],
    )[0]


def solution(mesh):
    placed = (P("seq", None), P("seq", None, "head"), P("head", "seq"), P("head", None), P("seq"))
    return jax.shard_map(
        per_device, mesh=mesh, in_specs=placed, out_specs=P("seq", "head"), check_vma=False
    )
```

```python
import functools
import math

import jax
import jax.numpy as jnp
from jax import lax
from jax.experimental import pallas as pl
from jax.experimental.pallas import tpu as pltpu
from jax.sharding import PartitionSpec as P

EPSILON = 1e-05
PAD = 16
VMEM_LIMIT = 50 * 1024 * 1024
NT = (((1,), (1,)), ((), ()))


def half_silu(t):
    return t * (1.0 + jnp.tanh(t))


def normalise(x):
    centre = x - jnp.mean(x, axis=-1, keepdims=True)
    spread = jnp.mean(centre * centre, axis=-1, keepdims=True)
    return centre * lax.rsqrt(spread + EPSILON)


def onehot_rows(stamp_row, buckets):
    count = stamp_row.shape[1]
    level = lax.broadcasted_iota(jnp.int32, (buckets, count), 0).astype(jnp.float32)
    return jnp.where(level == stamp_row, 1.0, 0.0).T


def vmem(count):
    return [pl.BlockSpec(memory_space=pltpu.VMEM)] * count


def norm_kernel(ids, events, normed_ref, half_ref):
    half = half_ref.shape[0]
    normed_ref[...] = normalise(events[...].astype(jnp.float32)).astype(jnp.bfloat16)
    half_ref[...] = normed_ref[pl.ds(pl.multiple_of(ids[2] * half, half), half), :]


def gather_weights(lead, lines, a, i, weights, wbuf, slices):
    size = wbuf.shape[1] // len(slices)
    chunk = wbuf.shape[0] // (lead * lines)
    for j in range(lines):
        for k in range(lead):
            place = ((a ^ k) * lines + (i ^ j)) * chunk
            to = pl.ds(pl.multiple_of(place, chunk), chunk)
            for n, part in enumerate(slices):
                wbuf[to, n * size : (n + 1) * size] = weights[j][
                    k * chunk : (k + 1) * chunk, part * size : (part + 1) * size
                ]


def keys_kernel(lead, lines, ids, normed, own_msg, *refs):
    arrived, refs = refs[: lead - 1], refs[lead - 1 :]
    others, refs = refs[: lead - 1], refs[lead - 1 :]
    marks, refs = refs[: lead - 1], refs[lead - 1 :]
    weights, (kv_ref, columns_ref, wbuf, all_ref) = refs[:lines], refs[lines:]
    a, i, c = ids[0], ids[1], ids[2]
    rows = normed.shape[0]
    half = rows // 2
    size = wbuf.shape[1] // 2
    chunk = wbuf.shape[0] // (lead * lines)
    gather_weights(lead, lines, a, i, weights, wbuf, (3, 1))
    for j in range(lines):
        columns_ref[j * chunk : (j + 1) * chunk, :] = weights[j][lead * chunk :, :]
    all_ref[pl.ds(pl.multiple_of(a * rows, rows), rows), :] = normed[...]
    for k in range(1, lead):
        for side, block in ((c, arrived[k - 1]), (1 - c, others[k - 1])):
            place = (a ^ k) * rows + side * half
            all_ref[pl.ds(pl.multiple_of(place, half), half), :] = block[...]
    for p in range(lead):
        block = slice(p * rows, (p + 1) * rows)
        product = jnp.dot(all_ref[block, :], wbuf[...], preferred_element_type=jnp.float32)
        kv_ref[block, :] = half_silu(0.5 * product).astype(jnp.bfloat16)
    stamp_rows = lax.broadcasted_iota(jnp.int32, (PAD, rows), 0)
    stamp_tile = jnp.zeros((PAD, rows), jnp.float32)
    for k, ref in enumerate((own_msg, *marks)):
        mark = ref[chunk : chunk + PAD, :rows].astype(jnp.float32)[0:1, :]
        stamp_tile = jnp.where(stamp_rows == (a ^ k), mark, stamp_tile)
    kv_ref[lead * rows :, :] = stamp_tile.astype(jnp.bfloat16)


def queries_kernel(lead, lines, ids, normed, time_bias, kv_ref, *refs):
    arrived, refs = refs[: lead - 1], refs[lead - 1 :]
    others, refs = refs[: lead - 1], refs[lead - 1 :]
    weights, (q_ref, *gate_refs, wbuf, ubuf, xbuf) = refs[:lines], refs[lines:]
    a, i, c = ids[0], ids[1], ids[2]
    size = wbuf.shape[1] // 2
    buckets = time_bias.shape[1]
    chunk = wbuf.shape[0] // (lead * lines)
    rows = normed.shape[0]
    half = rows // 2
    xbuf[pl.ds(pl.multiple_of(a * rows, rows), rows), :] = normed[...]
    for k in range(1, lead):
        for side, block in ((c, arrived[k - 1]), (1 - c, others[k - 1])):
            place = (a ^ k) * rows + side * half
            xbuf[pl.ds(pl.multiple_of(place, half), half), :] = block[...]
    gather_weights(lead, lines, a, i, weights, wbuf, (2, 0))
    bias = time_bias[...].astype(jnp.float32) * 0.5
    picked = lax.broadcasted_iota(jnp.int32, bias.shape, 0) == a
    bias = jnp.sum(jnp.where(picked, bias, 0.0), axis=0, keepdims=True)
    table = jnp.broadcast_to(bias, (buckets, buckets))
    table = pltpu.roll(table, 0, 1, stride=1, stride_axis=0).astype(jnp.bfloat16)
    marks = kv_ref[lead * rows :, :].astype(jnp.float32)
    scale = 0.5 / math.sqrt(size)
    for p in range(lead):
        block = slice(p * rows, (p + 1) * rows)
        product = jnp.dot(xbuf[block, :], wbuf[...], preferred_element_type=jnp.float32)
        active = half_silu(0.5 * product)
        q_ref[block, :size] = (active[:, :size] * scale).astype(jnp.bfloat16)
        ubuf[block, :] = active[:, size:].astype(jnp.bfloat16)
        chosen = onehot_rows(marks[p : p + 1, :], buckets).astype(jnp.bfloat16)
        q_ref[block, size:] = lax.dot_general(
            chosen, table, NT, preferred_element_type=jnp.float32
        ).astype(jnp.bfloat16)
    for k in range(lead):
        gate_refs[k][...] = ubuf[pl.ds(pl.multiple_of((a ^ k) * rows, rows), rows), :]


def attention_kernel(lead, j, last, pieces, ids, q_ref, *refs):
    refs = list(refs)
    kv_refs, refs = refs[:pieces], refs[pieces:]
    before = refs.pop(0) if j > 0 else None
    gates, refs = (refs[:lead], refs[lead:]) if last else ([], refs)
    outs, (kaug, values, total) = refs[:-3], refs[-3:]
    a, i = ids[0], ids[1]
    size = q_ref.shape[1] // 2
    rows = q_ref.shape[0] // lead
    buckets = q_ref.shape[1] - size
    span = lead * rows // pieces
    for n, ref in enumerate(kv_refs):
        kaug[n * span : (n + 1) * span, :size] = ref[:span, :size]
        if pieces > 1:
            values[n * span : (n + 1) * span, :] = ref[:span, size:]
    marks = kv_refs[-1][span:, :].astype(jnp.float32)
    for p in range(lead):
        kaug[p * rows : (p + 1) * rows, size:] = onehot_rows(marks[p : p + 1, :], buckets).astype(
            jnp.bfloat16
        )

    def visit(extra):
        for p in range(lead):
            block = slice(p * rows, (p + 1) * rows)
            count = (p + extra) * rows
            old = before[block, :] if before is not None else None
            if count == 0:
                total[block, :] = old if old is not None else jnp.zeros((rows, size), jnp.float32)
                continue
            t = lax.dot_general(
                q_ref[block, :], kaug[:count, :], NT, preferred_element_type=jnp.float32
            )
            weight = half_silu(t)
            if j == 0:
                row = lax.broadcasted_iota(jnp.int32, (rows, count), 0) + p * rows
                column = lax.broadcasted_iota(jnp.int32, (rows, count), 1)
                weight = jnp.where(column <= row, weight, 0.0)
            update = jnp.dot(
                weight.astype(jnp.bfloat16),
                values[:count, :] if pieces > 1 else kv_refs[0][:count, size:],
                preferred_element_type=jnp.float32,
            )
            total[block, :] = update if old is None else old + update

    if j == 0:
        visit(1)
    else:
        pl.when((i ^ j) < i)(lambda: visit(1))
        pl.when((i ^ j) > i)(lambda: visit(0))
    if last:
        for k in range(lead):
            base = pl.ds(pl.multiple_of((a ^ k) * rows, rows), rows)
            outs[k][:, :size] = total[base, :].astype(jnp.bfloat16)
            outs[k][:, size:] = gates[k][...]
    else:
        outs[0][...] = total[...]


def parcel_kernel(lead, lines, ids, *refs):
    columns, (kept_ref, give_ref) = refs[:lead], refs[lead:]
    a, i, c = ids[0], ids[1], ids[2]
    chunk = columns[0].shape[0] // lines
    parts = lead // 2

    def place(low_ref, high_ref):
        for n, ref in enumerate(columns):
            target = low_ref if n < parts else high_ref
            for j in range(lines):
                to = (((a ^ n) % parts) * lines + (i ^ j)) * chunk
                target[pl.ds(pl.multiple_of(to, chunk), chunk), :] = ref[
                    j * chunk : (j + 1) * chunk, :
                ]

    mine = a // parts == c
    pl.when(mine)(lambda: place(kept_ref, give_ref))
    pl.when(jnp.logical_not(mine))(lambda: place(give_ref, kept_ref))


def output_kernel(lead, ids, events, kept, given, *refs):
    own, refs = refs[:lead], refs[lead:]
    other, refs = refs[:lead], refs[lead:]
    out_ref, gated = refs
    a, c = ids[0], ids[2]
    rows, share = out_ref.shape
    size = own[0].shape[1] // 2
    full = 2 * lead * size
    parts = [ref[:, :size].astype(jnp.float32) for ref in (*own, *other)]
    middle = functools.reduce(jnp.add, [jnp.sum(x, -1, keepdims=True) for x in parts]) / full
    parts = [x - middle for x in parts]
    spread = functools.reduce(jnp.add, [jnp.sum(x * x, -1, keepdims=True) for x in parts]) / full
    inverse = lax.rsqrt(spread + EPSILON)
    for side, group in enumerate((own, other)):
        for k in range(lead):
            value = parts[side * lead + k] * inverse * group[k][:, size:].astype(jnp.float32)
            place = pl.ds(pl.multiple_of((a ^ k) * size, size), size)
            gated[side, :, place] = value.astype(jnp.bfloat16)
    total = lax.dot_general(gated[0], kept[...], NT, preferred_element_type=jnp.float32)
    total += lax.dot_general(gated[1], given[...], NT, preferred_element_type=jnp.float32)
    residual = events[:, pl.ds(pl.multiple_of(c * share, share), share)].astype(jnp.float32)
    out_ref[...] = (residual + total).astype(jnp.bfloat16)


def call(kernel, ins, outs, scratch):
    return list(pl.pallas_call(
        kernel,
        out_shape=outs,
        in_specs=[pl.BlockSpec(memory_space=pltpu.SMEM)] + vmem(len(ins) - 1),
        out_specs=vmem(len(outs)),
        scratch_shapes=scratch,
        compiler_params=pltpu.CompilerParams(vmem_limit_bytes=VMEM_LIMIT),
        cost_estimate=pl.CostEstimate(flops=1, bytes_accessed=1, transcendentals=0),
    )(*ins))


def per_device(events, w_uvqk, w_out, time_bias, stamps):
    bf16, f32 = jnp.bfloat16, jnp.float32
    devices = lax.axis_size("seq")
    rows, width = events.shape
    lead = time_bias.shape[0]
    lines = devices // lead
    chunk = w_uvqk.shape[0]
    size = w_uvqk.shape[2] // lead
    share = width // lax.axis_size("head")
    half = rows // 2
    place, c = lax.axis_index("seq"), lax.axis_index("head")
    a, i = place // lines, place % lines
    ids = jnp.stack([a, i, c]).astype(jnp.int32)

    def exchange(x, flip):
        return lax.ppermute(x, "seq", [(t, t ^ flip) for t in range(devices)])

    def swap(x):
        return lax.ppermute(x, "head", [(0, 1), (1, 0)])

    def shape(*dims, dtype=bf16):
        return jax.ShapeDtypeStruct(dims, dtype)

    by_head = w_uvqk.reshape(chunk, 4, lead, size).transpose(2, 0, 1, 3).reshape(lead, chunk, -1)
    stamp_rows = jnp.broadcast_to(stamps[None, :], (PAD, rows)).astype(bf16)
    stamp_rows = jnp.tile(stamp_rows, (1, -(-4 * size // rows)))[:, : 4 * size]
    sent = [
        jnp.concatenate([lax.dynamic_index_in_dim(by_head, a ^ k, 0, False), stamp_rows])
        for k in range(lead)
    ]
    got = [exchange(sent[k], k * lines) for k in range(1, lead)]
    normed, own_half = call(
        norm_kernel,
        [ids, events],
        [shape(rows, width), shape(half, width)],
        [],
    )
    own_half, got[0] = lax.optimization_barrier((own_half, got[0]))
    near, far = exchange(own_half, lines), exchange(own_half, 2 * lines)
    near, relayed = lax.optimization_barrier((near, far))
    arrived = [near, far, exchange(relayed, lines)]
    stack = jnp.concatenate([x[:chunk] for x in [sent[0], *got]] + [w_out.T])
    stacks = [stack] + [exchange(stack, j) for j in range(1, lines)]
    others = [swap(x) for x in arrived[:-1]]
    *stacks[1:], last_half = lax.optimization_barrier((*stacks[1:], arrived[-1]))
    arrived[-1] = last_half
    others.append(swap(last_half))

    span = lead * rows
    kv, columns = call(
        functools.partial(keys_kernel, lead, lines),
        [ids, normed, sent[0], *arrived, *others, *got, *stacks],
        [shape(span + PAD, 2 * size), shape(lines * chunk, w_out.shape[0])],
        [pltpu.VMEM((width, 2 * size), bf16), pltpu.VMEM((span, width), bf16)],
    )
    direct = [exchange(kv, j) for j in ((1, 2) if lines == 4 else range(1, lines))]
    near, far = exchange(columns, lines), exchange(columns, 2 * lines)
    queries, *gates = call(
        functools.partial(queries_kernel, lead, lines),
        [ids, normed, time_bias, kv, *arrived, *others, *stacks],
        [shape(span, size + time_bias.shape[1])] + [shape(rows, size)] * lead,
        [
            pltpu.VMEM((width, 2 * size), bf16),
            pltpu.VMEM((span, size), bf16),
            pltpu.VMEM((span, width), bf16),
        ],
    )

    def attend(j, total):
        last = j == lines - 1
        outs = [shape(rows, 2 * size)] * lead if last else [shape(span, size, dtype=f32)]
        return call(
            functools.partial(attention_kernel, lead, j, last, len(kvs[j])),
            [ids, queries, *kvs[j]] + ([total] if j else []) + (gates if last else []),
            outs,
            [
                pltpu.VMEM((span, queries.shape[1]), bf16),
                pltpu.VMEM((span, size), bf16),
                pltpu.VMEM((span, size), f32),
            ],
        )

    kvs = [[kv]] + [[x] for x in direct]
    result = attend(0, None)
    far, near, _ = lax.optimization_barrier((far, near, result[0]))
    *direct, result[0] = lax.optimization_barrier((*direct, result[0]))
    kvs = [[kv]] + [[x] for x in direct]
    if lines == 4:
        part = span // 2
        kvs.append([exchange(direct[1][:part], 1), exchange(direct[0][part:], 2)])
    relayed = exchange(far, lines)
    for j in range(1, lines):
        result = attend(j, result[0])
    relayed, result[0] = lax.optimization_barrier((relayed, result[0]))
    own = [result[0]] + [exchange(result[k], k * lines) for k in range(1, lead)]
    across = [swap(x) for x in own]
    parcel = shape(2 * lines * chunk, w_out.shape[0])
    kept, given = call(
        functools.partial(parcel_kernel, lead, lines),
        [ids, columns, near, far, relayed],
        [parcel, parcel],
        [],
    )
    given = swap(given)
    return call(
        functools.partial(output_kernel, lead),
        [ids, events, kept, given, *own, *across],
        [shape(rows, share)],
        [
            pltpu.VMEM((2, rows, lead * size), bf16),
        ],
    )[0]


def solution(mesh):
    placed = (P("seq", None), P("seq", None, "head"), P("head", "seq"), P("head", None), P("seq"))
    return jax.shard_map(
        per_device, mesh=mesh, in_specs=placed, out_specs=P("seq", "head"), check_vma=False
    )
```
